32 devices in a mesh: ep: 8 (over z, x), tp: 4 (over y, core).
Axes of the slice: x: 2, y: 2, z: 4, core: 2. Of those that a mesh axis runs over, the one named last changes fastest.
Arguments:
- tokens: bfloat16 [2048, 3072], P('ep', 'tp'), may hold values from -6 to 6
- routes: int32 [2048, 2], P('ep'), may hold values from 0 to 7, as said below
- route_gates: float32 [2048, 2], P('ep'), may hold values from 0.1 to 1
- up_weight: bfloat16 [8, 3072, 8192], P('ep', None, 'tp'), may hold values from -0.109375 to 0.109375
- down_weight: bfloat16 [8, 8192, 3072], P('ep', 'tp'), may hold values from -0.0625 to 0.0625
Outputs:
- layer_output: bfloat16 [2048, 3072], P('ep', 'tp')
The draws below stay inside these ranges and needn't reach their ends.
Inputs may be any that keep to these rules, and one draw needn't show every extreme that they name: `routes`: each row names two different experts. Among the 256 rows of one index of ep no expert is named more than 128 times, and one expert is named exactly 128 times by the rows of every index of ep.
All inputs are finite; a program needn't handle non-finite values.
Results may differ from the reference program's by a relative error of at most 0.019.
Values may be sent and summed in bfloat16 or wider, within the bound.
No kernel may reach another device: no remote copies, remote signals or barrier semaphores. Data moves between devices by JAX's collectives and lax.ppermute only.
A program may use at most 64 MiB of HBM per device.

```python
import jax
import jax.numpy as jnp
from jax import lax

D = 3072
FF = 8192
TOK_EP = 256
EXPERTS = 8
TOKENS = 2048
SLOT = 128
N_TP = 4


def draw_routes(key, part):
    mean_load = 2 * TOK_EP // EXPERTS
    hot_key, rest_key = jax.random.split(key)
    hot_expert = jax.random.randint(hot_key, (), 0, EXPERTS)
    places = jnp.arange(EXPERTS, dtype=jnp.int32)

    def one_block(block_key):
        order_key, moved_key, token_key, swap_key = jax.random.split(block_key, 4)
        expert_order = jax.random.permutation(order_key, EXPERTS).astype(jnp.int32)
        leading = expert_order[0]
        expert_order = jnp.where(expert_order == hot_expert, leading, expert_order)
        expert_order = jnp.where(places == 0, hot_expert, expert_order)
        moved_units = jax.random.randint(moved_key, (EXPERTS // 2,), 0, mean_load + 1)
        moved_units = jnp.where(places[:EXPERTS // 2] == 0, mean_load, moved_units)
        ordered = jnp.stack([mean_load + moved_units, mean_load - moved_units], axis=1).reshape(EXPERTS)
        counts = jnp.zeros((EXPERTS,), jnp.int32).at[expert_order].set(ordered.astype(jnp.int32))
        bounds = jnp.cumsum(counts)
        spots = jnp.arange(2 * TOK_EP, dtype=jnp.int32)
        labels = jnp.sum((spots[:, None] >= bounds[None, :]).astype(jnp.int32), axis=1)
        pair_table = jnp.stack([labels[:TOK_EP], labels[TOK_EP:]], axis=1)
        token_order = jax.random.permutation(token_key, TOK_EP)
        pair_table = pair_table[token_order]
        swap_mask = jax.random.randint(swap_key, (TOK_EP, 1), 0, 2)
        return jnp.where(swap_mask == 1, pair_table[:, ::-1], pair_table)
    block_keys = jax.random.split(rest_key, TOKENS // TOK_EP)
    return jax.vmap(one_block)(block_keys).reshape(TOKENS, 2).astype(jnp.int32)


def shard_levels(rng, shape, shards, low, largest):
    def one(axis_at, shards_of):
        steps = jax.random.uniform(jax.random.fold_in(jax.random.fold_in(rng, 6), axis_at), (shards_of,), jnp.float32, low / len(shards), largest / len(shards))
        return jnp.repeat(jnp.exp(steps), shape[axis_at] // shards_of).reshape((-1,) + (1,) * (len(shape) - axis_at - 1))

    loudness = one(*shards[0])
    for cut in shards[1:]:
        loudness = loudness * one(*cut)
    return loudness


def normal_values(own_key, dims, spread, limit, pieces=(), kind=jnp.bfloat16):
    loudness = shard_levels(own_key, dims, pieces, -0.22, 0.18) if pieces else 1.0
    array = jax.random.normal(own_key, dims, jnp.float32) * spread * loudness
    return jnp.minimum(jnp.maximum(array, -limit), limit).astype(kind)


def setup_inputs(seed: int = 0) -> dict:
    streams_of = jax.random.split(jax.random.key(seed), 6)
    return {
        "tokens": normal_values(streams_of[0], (TOKENS, D), 1.0, 6.0, ((0, 8), (1, 4))),
        "routes": draw_routes(jax.random.fold_in(streams_of[5], 71), 0),
        "route_gates": jnp.clip(0.1 + 0.9 * jax.random.uniform(streams_of[2], (TOKENS, 2), jnp.float32) ** shard_levels(streams_of[2], (TOKENS, 2), ((0, 8),), -0.2, 0.2), 0.1, 1.0),
        "up_weight": normal_values(streams_of[3], (EXPERTS, D, FF), D ** -0.5, 0.109375, ((0, 8), (2, 4))),
        "down_weight": normal_values(streams_of[4], (EXPERTS, FF, D), FF ** -0.5, 0.0625, ((0, 8), (1, 4))),
    }


def reference(tokens, routes, route_gates, up_weight, down_weight):
    flat_routes = routes.reshape(TOKENS * 2)
    member = (flat_routes[:, None] == jnp.arange(EXPERTS, dtype=jnp.int32)[None, :]).astype(jnp.int32)
    ranking = jnp.sum((jnp.cumsum(member, axis=0) - member) * member, axis=1).astype(jnp.int32)
    capacity = EXPERTS * SLOT
    owners = (jnp.arange(TOKENS * 2, dtype=jnp.int32) // 2).astype(jnp.int32)
    row_table = jnp.zeros((EXPERTS, capacity), jnp.int32).at[flat_routes, ranking].set(owners)
    block_width = FF // N_TP

    def expert_rows(expert_index):
        chosen = tokens[row_table[expert_index]]
        raised = jnp.dot(chosen, up_weight[expert_index], preferred_element_type=jnp.float32)
        hidden = jax.nn.silu(raised).astype(jnp.bfloat16)
        running = jnp.zeros((capacity, D), jnp.float32)
        for block_index in range(N_TP):
            low = block_index * block_width
            portion = jnp.dot(hidden[:, low:low + block_width], down_weight[expert_index, low:low + block_width, :], preferred_element_type=jnp.float32)
            rounded = lax.optimization_barrier(portion.astype(jnp.bfloat16))
            running = running + rounded.astype(jnp.float32)
        return running.astype(jnp.bfloat16)

    outputs = lax.map(expert_rows, jnp.arange(EXPERTS, dtype=jnp.int32))
    outputs = outputs.reshape(EXPERTS * capacity, D)
    ranks = ranking.reshape(TOKENS, 2)
    first_pick = outputs[routes[:, 0] * capacity + ranks[:, 0]].astype(jnp.float32)
    second_pick = outputs[routes[:, 1] * capacity + ranks[:, 1]].astype(jnp.float32)
    combined = route_gates[:, 0:1] * first_pick + route_gates[:, 1:2] * second_pick
    return combined.astype(jnp.bfloat16)
```

```python
import functools

import jax
import jax.numpy as jnp
from jax import lax
from jax.experimental import pallas as pl
from jax.experimental.pallas import tpu as pltpu
from jax.sharding import PartitionSpec as P

BF16 = jnp.bfloat16
F32 = jnp.float32


def pick_kernel(places, me, slot, routes_ref, tokens_ref, target_ref, *row_refs):
    count = routes_ref.shape[0]
    first, second = routes_ref[:, 0:1], routes_ref[:, 1:2]
    expert = lax.broadcasted_iota(jnp.int32, (count, 128), 1)
    is_first, is_second = expert == first, expert == second
    member = (is_first | is_second).astype(F32).astype(BF16)
    earlier = (
        lax.broadcasted_iota(jnp.int32, (count, count), 1) < lax.broadcasted_iota(jnp.int32, (count, count), 0)
    ).astype(F32).astype(BF16)
    before = jnp.dot(earlier, member, preferred_element_type=F32).astype(jnp.int32)
    index = me[0]
    high = (expert >> 1) - (index >> 1)
    place = jnp.where(high < 0, high + places // 2, high) * 2 + ((expert + index) & 1)
    spot = place * slot + before
    target_first = jnp.sum(jnp.where(is_first, spot, 0), axis=1, keepdims=True)
    target_second = jnp.sum(jnp.where(is_second, spot, 0), axis=1, keepdims=True)
    target_ref[:, 0:1] = target_first
    target_ref[:, 1:2] = target_second
    tokens = tokens_ref[...]
    for r in range(places):
        lane = lax.broadcasted_iota(jnp.int32, (count, slot), 1) + r * slot
        chosen = ((lane == target_first) | (lane == target_second)).astype(F32).astype(BF16)
        rows = lax.dot_general(chosen, tokens, (((0,), (0,)), ((), ())), preferred_element_type=F32)
        row_refs[r][...] = rows.astype(BF16)


def pick_rows(routes, tokens, me, slot, places):
    count, width = tokens.shape
    vmem = pl.BlockSpec(memory_space=pltpu.VMEM)

    def body(me_ref, *refs):
        pick_kernel(places, me_ref, slot, *refs)

    return pl.pallas_call(
        body,
        in_specs=[pl.BlockSpec(memory_space=pltpu.SMEM), vmem, vmem],
        out_specs=[vmem] * (places + 1),
        out_shape=[jax.ShapeDtypeStruct((count, 2), jnp.int32)]
        + [jax.ShapeDtypeStruct((slot, width), BF16)] * places,
        compiler_params=pltpu.CompilerParams(vmem_limit_bytes=32 << 20),
        cost_estimate=pl.CostEstimate(flops=2 * count * slot * places * width, bytes_accessed=4 << 20, transcendentals=0),
        name="pick_rows",
    )(me, routes, tokens)


def combine_rows(target, gates, returned, slot):
    count = target.shape[0]
    width = returned[0].shape[1]
    vmem = pl.BlockSpec(memory_space=pltpu.VMEM)

    def body(target_ref, gates_ref, *refs):
        out_ref = refs[-1]
        total = None
        for k in range(2):
            picked = None
            for r, rows_ref in enumerate(refs[:-1]):
                lane = lax.broadcasted_iota(jnp.int32, (count, slot), 1) + r * slot
                chosen = (lane == target_ref[:, k : k + 1]).astype(F32).astype(BF16)
                part = jnp.dot(chosen, rows_ref[...], preferred_element_type=F32)
                picked = part if picked is None else picked + part
            weighted = gates_ref[:, k : k + 1] * picked
            total = weighted if total is None else total + weighted
        out_ref[...] = total.astype(BF16)

    return pl.pallas_call(
        body,
        in_specs=[vmem] * (2 + len(returned)),
        out_specs=vmem,
        out_shape=jax.ShapeDtypeStruct((count, width), BF16),
        compiler_params=pltpu.CompilerParams(vmem_limit_bytes=32 << 20),
        cost_estimate=pl.CostEstimate(
            flops=4 * count * slot * len(returned) * width, bytes_accessed=4 << 20, transcendentals=0
        ),
        name="combine_rows",
    )(target, gates, *returned)


def feed_forward(order, pieces, up, down, hidden_block):
    n = len(pieces)
    rows, width = pieces[0].shape
    hidden, features = down.shape
    steps = hidden // hidden_block
    half = n // 2

    def body(order_ref, *refs):
        piece_refs, up_refs, down_ref = refs[:n], refs[n : 2 * n], refs[2 * n]
        near_refs, far_ref, total = refs[2 * n + 1 : 2 * n + 1 + half], refs[-2], refs[-1]
        step = pl.program_id(0)
        raised = None
        for piece_ref, up_ref in zip(piece_refs, up_refs):
            part = jnp.dot(piece_ref[...], up_ref[...], preferred_element_type=F32)
            raised = part if raised is None else raised + part
        active = (raised / (1.0 + jnp.exp(-raised))).astype(BF16)
        lowered = jnp.dot(active, down_ref[...], preferred_element_type=F32)

        @pl.when(step == 0)
        def _():
            total[...] = lowered

        @pl.when(step > 0)
        def _():
            total[...] += lowered

        @pl.when(step == steps - 1)
        def _():
            for i in range(n):
                start = pl.multiple_of(order_ref[i] * width, 128)
                value = total[:, pl.ds(start, width)].astype(BF16)
                if i < half:
                    near_refs[i][...] = value
                else:
                    far_ref[i - half] = value

    def up_spec(i):
        return pl.BlockSpec((width, hidden_block), lambda s, order_ref: (order_ref[i], s))

    whole = pl.BlockSpec((rows, width), lambda s, order_ref: (0, 0))
    return pl.pallas_call(
        body,
        grid_spec=pltpu.PrefetchScalarGridSpec(
            num_scalar_prefetch=1,
            grid=(steps,),
            in_specs=[whole] * n
            + [up_spec(i) for i in range(n)]
            + [pl.BlockSpec((hidden_block, features), lambda s, order_ref: (s, 0))],
            out_specs=[whole] * half + [pl.BlockSpec((half, rows, width), lambda s, order_ref: (0, 0, 0))],
            scratch_shapes=[pltpu.VMEM((rows, features), F32)],
        ),
        out_shape=[jax.ShapeDtypeStruct((rows, width), BF16)] * half
        + [jax.ShapeDtypeStruct((half, rows, width), BF16)],
        compiler_params=pltpu.CompilerParams(vmem_limit_bytes=48 << 20),
        cost_estimate=pl.CostEstimate(
            flops=4 * rows * hidden * features,
            bytes_accessed=4 * hidden * features + 4 * rows * features,
            transcendentals=rows * hidden,
        ),
        name="feed_forward",
    )(order, *pieces, *([up] * n), down)


def per_device(tokens, routes, route_gates, up_weight, down_weight):
    places, ranks = lax.axis_size("ep"), lax.axis_size("tp")
    count = tokens.shape[0]
    slot = 4 * count // places
    layers, planes = places // 2, ranks // 2
    group = max(1, min(layers, 256 // (2 * slot)))
    up, down = up_weight[0], down_weight[0]
    me, rank = lax.axis_index("ep"), lax.axis_index("tp")

    def ep_hop(value, place, back=False):
        far, flip = place // 2, place % 2
        pairs = [(i, (i // 2 + far) % layers * 2 + (i % 2 ^ flip)) for i in range(places)]
        return lax.ppermute(value, "ep", [(b, a) for a, b in pairs] if back else pairs)

    def plane_hop(value, far):
        return lax.ppermute(value, "tp", [(i, (i // 2 + far) % planes * 2 + i % 2) for i in range(ranks)])

    def core_hop(value):
        return lax.ppermute(value, "tp", [(i, i ^ 1) for i in range(ranks)])

    order = jnp.stack(
        [(rank // 2 - far) % planes * 2 + rank % 2 for far in range(planes)]
        + [(rank // 2 - far) % planes * 2 + (1 - rank % 2) for far in range(planes)]
    ).astype(jnp.int32)
    target, *picked = pick_rows(routes, tokens, me.reshape(1).astype(jnp.int32), slot, places)
    returned = [None] * places
    arrived = [picked[0]] + [ep_hop(picked[place], place) for place in range(1, places)]
    for chunk in range(layers // group):
        members = range(chunk * 2 * group, (chunk + 1) * 2 * group)
        own = jnp.concatenate([arrived[place] for place in members], axis=0)
        same_core = [own] + [plane_hop(own, far) for far in range(1, planes)]
        other_core = [core_hop(piece) for piece in same_core]
        *near, stacked = feed_forward(order, same_core + other_core, up, down, 256)
        crossed = core_hop(stacked)
        summed = near[0].astype(F32) + crossed[0].astype(F32)
        for far in range(1, planes):
            outgoing = (near[far].astype(F32) + crossed[far].astype(F32)).astype(BF16)
            summed = summed + plane_hop(outgoing, planes - far).astype(F32)
        for i, place in enumerate(members):
            result = summed[i * slot : (i + 1) * slot].astype(BF16)
            returned[place] = result if place == 0 else ep_hop(result, place, back=True)
    return combine_rows(target, route_gates, returned, slot)


def solution(mesh):
    in_specs = (
        P("ep", "tp"),
        P("ep", None),
        P("ep", None),
        P("ep", None, "tp"),
        P("ep", "tp", None),
    )
    out_specs = P("ep", "tp")
    return jax.shard_map(
        per_device, mesh=mesh, in_specs=in_specs, out_specs=out_specs, check_vma=False
    )
```

```python
import functools

import jax
import jax.numpy as jnp
from jax import lax
from jax.experimental import pallas as pl
from jax.experimental.pallas import tpu as pltpu
from jax.sharding import PartitionSpec as P

BF16 = jnp.bfloat16
F32 = jnp.float32
FREE = pl.CostEstimate(flops=0, bytes_accessed=0, transcendentals=0)


def pick_kernel(places, me, slot, routes_ref, tokens_ref, target_ref, *row_refs):
    count = routes_ref.shape[0]
    first, second = routes_ref[:, 0:1], routes_ref[:, 1:2]
    expert = lax.broadcasted_iota(jnp.int32, (count, 128), 1)
    is_first, is_second = expert == first, expert == second
    member = (is_first | is_second).astype(F32).astype(BF16)
    earlier = (
        lax.broadcasted_iota(jnp.int32, (count, count), 1) < lax.broadcasted_iota(jnp.int32, (count, count), 0)
    ).astype(F32).astype(BF16)
    before = jnp.dot(earlier, member, preferred_element_type=F32).astype(jnp.int32)
    index = me[0]
    high = (expert >> 1) - (index >> 1)
    place = jnp.where(high < 0, high + places // 2, high) * 2 + ((expert + index) & 1)
    spot = place * slot + before
    target_first = jnp.sum(jnp.where(is_first, spot, 0), axis=1, keepdims=True)
    target_second = jnp.sum(jnp.where(is_second, spot, 0), axis=1, keepdims=True)
    target_ref[:, 0:1] = target_first
    target_ref[:, 1:2] = target_second
    tokens = tokens_ref[...]
    for r in range(places):
        lane = lax.broadcasted_iota(jnp.int32, (count, slot), 1) + r * slot
        chosen = ((lane == target_first) | (lane == target_second)).astype(F32).astype(BF16)
        rows = lax.dot_general(chosen, tokens, (((0,), (0,)), ((), ())), preferred_element_type=F32)
        row_refs[r][...] = rows.astype(BF16)


def pick_rows(routes, tokens, me, slot, places):
    count, width = tokens.shape
    vmem = pl.BlockSpec(memory_space=pltpu.VMEM)

    def body(me_ref, *refs):
        pick_kernel(places, me_ref, slot, *refs)

    return pl.pallas_call(
        body,
        in_specs=[pl.BlockSpec(memory_space=pltpu.SMEM), vmem, vmem],
        out_specs=[vmem] * (places + 1),
        out_shape=[jax.ShapeDtypeStruct((count, 2), jnp.int32)]
        + [jax.ShapeDtypeStruct((slot, width), BF16)] * places,
        compiler_params=pltpu.CompilerParams(vmem_limit_bytes=24 << 20),
        cost_estimate=FREE,
        name="pick_rows",
    )(me, routes, tokens)


def combine_rows(target, gates, returned, slot):
    count = target.shape[0]
    width = returned[0].shape[1]
    vmem = pl.BlockSpec(memory_space=pltpu.VMEM)

    def body(target_ref, gates_ref, *refs):
        out_ref = refs[-1]
        total = None
        for k in range(2):
            picked = None
            for r, rows_ref in enumerate(refs[:-1]):
                lane = lax.broadcasted_iota(jnp.int32, (count, slot), 1) + r * slot
                chosen = (lane == target_ref[:, k : k + 1]).astype(F32).astype(BF16)
                part = jnp.dot(chosen, rows_ref[...], preferred_element_type=F32)
                picked = part if picked is None else picked + part
            weighted = gates_ref[:, k : k + 1] * picked
            total = weighted if total is None else total + weighted
        out_ref[...] = total.astype(BF16)

    return pl.pallas_call(
        body,
        in_specs=[vmem] * (2 + len(returned)),
        out_specs=vmem,
        out_shape=jax.ShapeDtypeStruct((count, width), BF16),
        compiler_params=pltpu.CompilerParams(vmem_limit_bytes=24 << 20),
        cost_estimate=FREE,
        name="combine_rows",
    )(target, gates, *returned)


def load(weights, after):
    n = len(weights)

    def body(*refs):
        copies = [pltpu.make_async_copy(refs[i], refs[n + 1 + i], refs[-1].at[i]) for i in range(n)]
        for copy in copies:
            copy.start()
        for copy in copies:
            copy.wait()

    return pl.pallas_call(
        body,
        in_specs=[pl.BlockSpec(memory_space=pltpu.HBM)] * n + [pl.BlockSpec(memory_space=pl.ANY)],
        out_specs=[pl.BlockSpec(memory_space=pltpu.VMEM)] * n,
        out_shape=[pltpu.VMEM(one.shape, one.dtype) for one in weights],
        scratch_shapes=[pltpu.SemaphoreType.DMA((n,))],
        compiler_params=pltpu.CompilerParams(vmem_limit_bytes=24 << 20),
        cost_estimate=FREE,
        name="load_weights",
    )(*[pltpu.with_memory_space_constraint(one, pltpu.HBM) for one in weights], after)


def feed_forward(order, pieces, up, down, after):
    n, waits = len(pieces), len(after)
    blocks = [len(piece) for piece in pieces]
    flat = [block for piece in pieces for block in piece]
    rows, width = sum(block.shape[0] for block in pieces[0]), flat[0].shape[1]
    hidden, features = down.shape
    half = n // 2

    def body(order_ref, *refs):
        piece_refs, up_ref, down_ref = list(refs[: len(flat)]), refs[len(flat)], refs[len(flat) + 1]
        near_refs, (far_ref, arrived, active) = refs[len(flat) + 2 + waits : -3], refs[-3:]
        starts = [pl.multiple_of(order_ref[i] * width, 128) for i in range(n)]
        for i in range(n):
            at = 0
            for _ in range(blocks[i]):
                block = piece_refs.pop(0)
                arrived[at : at + block.shape[0], pl.ds(starts[i], width)] = block[...]
                at += block.shape[0]
        raised = jnp.dot(arrived[...], up_ref[...], preferred_element_type=F32)
        active[...] = (0.5 * raised * (1.0 + jnp.tanh(0.5 * raised))).astype(BF16)
        for i in reversed(range(n)):
            value = jnp.dot(active[...], down_ref[:, pl.ds(starts[i], width)], preferred_element_type=F32)
            if i < half:
                near_refs[i][...] = value.astype(BF16)
            else:
                far_ref[i - half] = value.astype(BF16)

    vmem = pl.BlockSpec(memory_space=pltpu.VMEM)
    return pl.pallas_call(
        body,
        in_specs=[pl.BlockSpec(memory_space=pltpu.SMEM)]
        + [vmem] * (len(flat) + 2)
        + [pl.BlockSpec(memory_space=pl.ANY)] * waits,
        out_specs=[vmem] * (half + 1),
        scratch_shapes=[pltpu.VMEM((rows, features), BF16), pltpu.VMEM((rows, hidden), BF16)],
        out_shape=[jax.ShapeDtypeStruct((rows, width), BF16)] * half
        + [jax.ShapeDtypeStruct((half, rows, width), BF16)],
        compiler_params=pltpu.CompilerParams(vmem_limit_bytes=16 << 20),
        cost_estimate=FREE,
        name="feed_forward",
    )(order, *flat, *[pltpu.with_memory_space_constraint(one, pltpu.VMEM) for one in (up, down)], *after)


class Lane:
    def __init__(self, depth):
        self.depth, self.ended = depth, []

    def send(self, hop, *values):
        if len(self.ended) >= self.depth:
            values = lax.optimization_barrier((*values, *self.ended[-self.depth]))[: len(values)]
        self.ended.append([hop(value) if callable(hop) else hop[i](value) for i, value in enumerate(values)])
        return self.ended[-1]


def per_device(tokens, routes, route_gates, up_weight, down_weight):
    places, ranks = lax.axis_size("ep"), lax.axis_size("tp")
    count = tokens.shape[0]
    slot = 4 * count // places
    layers, planes = places // 2, ranks // 2
    group = max(1, min(layers, 256 // (2 * slot)))
    chunks = layers // group
    members = [range(chunk * 2 * group, (chunk + 1) * 2 * group) for chunk in range(chunks)]
    me, rank = lax.axis_index("ep"), lax.axis_index("tp")

    def ep_hop(place, back=False):
        far, flip = place // 2, place % 2
        pairs = [(i, (i // 2 + far) % layers * 2 + (i % 2 ^ flip)) for i in range(places)]
        return lambda value: lax.ppermute(value, "ep", [(b, a) for a, b in pairs] if back else pairs)

    def plane_hop(far):
        pairs = [(i, (i // 2 + far) % planes * 2 + i % 2) for i in range(ranks)]
        return lambda value: lax.ppermute(value, "tp", pairs)

    def core_hop(value):
        return lax.ppermute(value, "tp", [(i, i ^ 1) for i in range(ranks)])

    def gather(value):
        return plane_lane.send([plane_hop(far) for far in range(1, planes)], *[value] * (planes - 1))

    def join(values):
        return values[0] if len(values) == 1 else jnp.concatenate(values, axis=0)

    plane_lane, out_lane, back_lane = Lane(2), Lane(1), Lane(2)
    order = jnp.stack(
        [(rank // 2 - far) % planes * 2 + rank % 2 for far in range(planes)]
        + [(rank // 2 - far) % planes * 2 + (1 - rank % 2) for far in range(planes)]
    ).astype(jnp.int32)
    target, *picked = pick_rows(routes, tokens, me.reshape(1).astype(jnp.int32), slot, places)
    pieces, returned = [None] * chunks, [None] * places

    def fetch(chunk):
        places_of = [place for place in members[chunk] if place > 0]
        rows = [picked[place] for place in places_of]
        return out_lane.send([ep_hop(place) for place in places_of], *rows)

    def spread(chunk, own, across):
        same_core = [own, *across]
        pieces[chunk] = [[piece] for piece in same_core + [core_hop(piece) for piece in same_core]]

    def work(chunk):
        *near, stacked = feed_forward(order, pieces[chunk], up, down, [])
        crossed = core_hop(stacked)
        outgoing = [(near[far].astype(F32) + crossed[far].astype(F32)).astype(BF16) for far in range(1, planes)]
        summed = near[0].astype(F32) + crossed[0].astype(F32)
        for part in plane_lane.send([plane_hop(planes - far) for far in range(1, planes)], *outgoing):
            summed = summed + part.astype(F32)
        results = [summed[i * slot : (i + 1) * slot].astype(BF16) for i in range(len(members[chunk]))]
        if chunk == 0:
            returned[0] = results.pop(0)
        away = [place for place in members[chunk] if place > 0]
        for place, result in zip(away, back_lane.send([ep_hop(place, back=True) for place in away], *results)):
            returned[place] = result

    home = gather(picked[0])
    first, out_lane = fetch(0), Lane(1)
    across = gather(join(first))
    own = jnp.concatenate([picked[0], *first], axis=0)
    spread(0, own, [jnp.concatenate(pair, axis=0) for pair in zip(home, across)])
    for chunk in range(chunks):
        if chunk + 1 < chunks:
            own = join(fetch(chunk + 1))
            if chunk == 0:
                up, down = load([up_weight[0], down_weight[0]], own)
                spread(1, own, gather(own))
                work(0)
            else:
                spread(chunk + 1, own, gather(own))
                work(chunk)
        else:
            work(chunk)
    return combine_rows(target, route_gates, returned, slot)


def solution(mesh):
    in_specs = (
        P("ep", "tp"),
        P("ep", None),
        P("ep", None),
        P("ep", None, "tp"),
        P("ep", "tp", None),
    )
    out_specs = P("ep", "tp")
    return jax.shard_map(
        per_device, mesh=mesh, in_specs=in_specs, out_specs=out_specs, check_vma=False
    )
```

```python
import functools

import jax
import jax.numpy as jnp
from jax import lax
from jax.experimental import pallas as pl
from jax.experimental.pallas import tpu as pltpu
from jax.sharding import PartitionSpec as P

BF16 = jnp.bfloat16
F32 = jnp.float32
FREE = pl.CostEstimate(flops=0, bytes_accessed=0, transcendentals=0)

TIES = {
    "k3": ("k2", "y1"),
    "y1": ("own", "p0"),
    "Y0": ("p0",),
    "y2": ("y1",),
    "Y1": ("Y0",),
    "y3": ("y2",),
    "Y2": ("Y1",),
    "Y3": ("y3",),
    "Z2": ("Z0",),
    "Z3": ("Z1",),
    "k2": ("k0",),
}


def pick_kernel(places, me, slot, routes_ref, tokens_ref, target_ref, *row_refs):
    count = routes_ref.shape[0]
    first, second = routes_ref[:, 0:1], routes_ref[:, 1:2]
    expert = lax.broadcasted_iota(jnp.int32, (count, 128), 1)
    is_first, is_second = expert == first, expert == second
    member = (is_first | is_second).astype(F32).astype(BF16)
    earlier = (
        lax.broadcasted_iota(jnp.int32, (count, count), 1) < lax.broadcasted_iota(jnp.int32, (count, count), 0)
    ).astype(F32).astype(BF16)
    before = jnp.dot(earlier, member, preferred_element_type=F32).astype(jnp.int32)
    index = me[0]
    high = (expert >> 1) - (index >> 1)
    place = jnp.where(high < 0, high + places // 2, high) * 2 + ((expert + index) & 1)
    spot = place * slot + before
    target_first = jnp.sum(jnp.where(is_first, spot, 0), axis=1, keepdims=True)
    target_second = jnp.sum(jnp.where(is_second, spot, 0), axis=1, keepdims=True)
    target_ref[:, 0:1] = target_first
    target_ref[:, 1:2] = target_second
    tokens = tokens_ref[...]
    for r in range(places):
        lane = lax.broadcasted_iota(jnp.int32, (count, slot), 1) + r * slot
        chosen = ((lane == target_first) | (lane == target_second)).astype(F32).astype(BF16)
        rows = lax.dot_general(chosen, tokens, (((0,), (0,)), ((), ())), preferred_element_type=F32)
        row_refs[r][...] = rows.astype(BF16)


def pick_rows(routes, tokens, me, slot, places):
    count, width = tokens.shape
    vmem = pl.BlockSpec(memory_space=pltpu.VMEM)

    def body(me_ref, *refs):
        pick_kernel(places, me_ref, slot, *refs)

    return pl.pallas_call(
        body,
        in_specs=[pl.BlockSpec(memory_space=pltpu.SMEM), vmem, vmem],
        out_specs=[vmem] * (places + 1),
        out_shape=[jax.ShapeDtypeStruct((count, 2), jnp.int32)]
        + [jax.ShapeDtypeStruct((slot, width), BF16)] * places,
        compiler_params=pltpu.CompilerParams(vmem_limit_bytes=24 << 20),
        cost_estimate=FREE,
        name="pick_rows",
    )(me, routes, tokens)


def combine_rows(target, gates, returned, slot):
    count = target.shape[0]
    width = returned[0].shape[1]
    vmem = pl.BlockSpec(memory_space=pltpu.VMEM)

    def body(target_ref, gates_ref, *refs):
        out_ref = refs[-1]
        total = None
        for k in range(2):
            picked = None
            for r, rows_ref in enumerate(refs[:-1]):
                lane = lax.broadcasted_iota(jnp.int32, (count, slot), 1) + r * slot
                chosen = (lane == target_ref[:, k : k + 1]).astype(F32).astype(BF16)
                part = jnp.dot(chosen, rows_ref[...], preferred_element_type=F32)
                picked = part if picked is None else picked + part
            weighted = gates_ref[:, k : k + 1] * picked
            total = weighted if total is None else total + weighted
        out_ref[...] = total.astype(BF16)

    return pl.pallas_call(
        body,
        in_specs=[vmem] * (2 + len(returned)),
        out_specs=vmem,
        out_shape=jax.ShapeDtypeStruct((count, width), BF16),
        compiler_params=pltpu.CompilerParams(vmem_limit_bytes=24 << 20),
        cost_estimate=FREE,
        name="combine_rows",
    )(target, gates, *returned)


def load(weights, after):
    n = len(weights)

    def body(*refs):
        copies = [pltpu.make_async_copy(refs[i], refs[n + 1 + i], refs[-1].at[i]) for i in range(n)]
        for copy in copies:
            copy.start()
        for copy in copies:
            copy.wait()

    return pl.pallas_call(
        body,
        in_specs=[pl.BlockSpec(memory_space=pltpu.HBM)] * n + [pl.BlockSpec(memory_space=pl.ANY)],
        out_specs=[pl.BlockSpec(memory_space=pltpu.VMEM)] * n,
        out_shape=[pltpu.VMEM(one.shape, one.dtype) for one in weights],
        scratch_shapes=[pltpu.SemaphoreType.DMA((n,))],
        compiler_params=pltpu.CompilerParams(vmem_limit_bytes=24 << 20),
        cost_estimate=FREE,
        name="load_weights",
    )(*[pltpu.with_memory_space_constraint(one, pltpu.HBM) for one in weights], after)


def feed_forward(order, near, far, up, down):
    planes = len(near)
    rows, width = near[0].shape
    hidden, features = down.shape

    def body(order_ref, *refs):
        piece_refs, up_ref, down_ref = refs[: 2 * planes], refs[2 * planes], refs[2 * planes + 1]
        to_near_refs, (to_far_ref, arrived, active) = refs[2 * planes + 2 : -3], refs[-3:]
        starts = [pl.multiple_of(order_ref[i] * width, 128) for i in range(2 * planes)]
        for start, piece_ref in zip(starts, piece_refs):
            arrived[:, pl.ds(start, width)] = piece_ref[...]
        raised = jnp.dot(arrived[...], up_ref[...], preferred_element_type=F32)
        active[...] = (0.5 * raised * (1.0 + jnp.tanh(0.5 * raised))).astype(BF16)
        for i in reversed(range(2 * planes)):
            value = jnp.dot(active[...], down_ref[:, pl.ds(starts[i], width)], preferred_element_type=F32)
            if i < planes:
                to_near_refs[i][...] = value.astype(BF16)
            else:
                to_far_ref[i - planes] = value.astype(BF16)

    vmem = pl.BlockSpec(memory_space=pltpu.VMEM)
    out_shape = [jax.ShapeDtypeStruct((rows, width), BF16)] * planes
    out_shape.append(jax.ShapeDtypeStruct((planes, rows, width), BF16))
    return pl.pallas_call(
        body,
        in_specs=[pl.BlockSpec(memory_space=pltpu.SMEM)]
        + [vmem] * (2 * planes + 2),
        out_specs=[vmem] * len(out_shape),
        scratch_shapes=[pltpu.VMEM((rows, features), BF16), pltpu.VMEM((rows, hidden), BF16)],
        out_shape=out_shape,
        compiler_params=pltpu.CompilerParams(vmem_limit_bytes=16 << 20),
        cost_estimate=pl.CostEstimate(
            flops=4 * rows * hidden * features, bytes_accessed=0, transcendentals=0
        ),
        name="feed_forward",
    )(order, *near, *far, *[pltpu.with_memory_space_constraint(one, pltpu.VMEM) for one in (up, down)])


class Events:
    def __init__(self):
        self.values = {}

    def after(self, name):
        return [one for event in TIES.get(name, ()) for one in self.values.get(event, [])]

    def hold(self, name, values):
        after = self.after(name)
        return list(lax.optimization_barrier((*values, *after))[: len(values)]) if after else list(values)


def per_device(tokens, routes, route_gates, up_weight, down_weight):
    places, ranks = lax.axis_size("ep"), lax.axis_size("tp")
    count = tokens.shape[0]
    slot = 4 * count // places
    layers, planes = places // 2, ranks // 2
    group = max(1, min(layers, 256 // (2 * slot)))
    chunks = layers // group
    members = [range(chunk * 2 * group, (chunk + 1) * 2 * group) for chunk in range(chunks)]
    me, rank = lax.axis_index("ep"), lax.axis_index("tp")
    events = Events()

    def ep_hop(value, place, back=False):
        far, flip = place // 2, place % 2
        pairs = [(i, (i // 2 + far) % layers * 2 + (i % 2 ^ flip)) for i in range(places)]
        return lax.ppermute(value, "ep", [(b, a) for a, b in pairs] if back else pairs)

    def plane_hop(value, far):
        return lax.ppermute(value, "tp", [(i, (i // 2 + far) % planes * 2 + i % 2) for i in range(ranks)])

    def core_hop(value):
        return lax.ppermute(value, "tp", [(i, i ^ 1) for i in range(ranks)])

    def gather(name, value):
        held = events.hold(name, [value])[0]
        events.values[name] = [plane_hop(held, far) for far in range(1, planes)]
        return events.values[name]

    def join(values):
        return values[0] if len(values) == 1 else jnp.concatenate(values, axis=0)

    def fetch(name, chunk):
        away = [place for place in members[chunk] if place > 0]
        held = events.hold(name, [picked[place] for place in away])
        events.values[name] = [ep_hop(value, place) for value, place in zip(held, away)]
        return events.values[name]

    order = jnp.stack(
        [(rank // 2 - far) % planes * 2 + rank % 2 for far in range(planes)]
        + [(rank // 2 - far) % planes * 2 + (1 - rank % 2) for far in range(planes)]
    ).astype(jnp.int32)
    target, *picked = pick_rows(routes, tokens, me.reshape(1).astype(jnp.int32), slot, places)
    pieces, totals, outs, returned = [None] * chunks, [None] * chunks, [None] * chunks, [None] * places

    def spread(chunk, own, across):
        same_core = [own, *across]
        pieces[chunk] = (same_core, [core_hop(piece) for piece in same_core])

    def work(chunk):
        *near, stacked = feed_forward(order, *pieces[chunk], up, down)
        crossed = core_hop(stacked)
        outs[chunk] = [(near[far].astype(F32) + crossed[far].astype(F32)).astype(BF16) for far in range(1, planes)]
        totals[chunk] = near[0].astype(F32) + crossed[0].astype(F32)

    def reduce(chunk):
        held = events.hold(f"Y{chunk}", outs[chunk])
        got = [plane_hop(one, planes - far) for far, one in enumerate(held, 1)]
        events.values[f"Y{chunk}"] = got
        for part in got:
            totals[chunk] = totals[chunk] + part.astype(F32)

    def give(chunk):
        results = [totals[chunk][i * slot : (i + 1) * slot].astype(BF16) for i in range(len(members[chunk]))]
        away = [place for place in members[chunk] if place > 0]
        if chunk == 0:
            returned[0] = results.pop(0)
        held = events.hold(f"Z{chunk}", results)
        events.values[f"Z{chunk}"] = [ep_hop(one, place, back=True) for one, place in zip(held, away)]
        for place, one in zip(away, events.values[f"Z{chunk}"]):
            returned[place] = one

    home = gather("own", picked[0])
    first = fetch("k0", 0)
    fetched = {1: join(fetch("k1", 1))}
    across = gather("p0", join(first))
    up, down = load([up_weight[0], down_weight[0]], events.values["k1"][0])
    spread(0, join([picked[0], *first]), [join(pair) for pair in zip(home, across)])
    for chunk in range(chunks):
        if chunk + 2 < chunks:
            fetched[chunk + 2] = join(fetch(f"k{chunk + 2}", chunk + 2))
        if chunk + 1 < chunks:
            spread(chunk + 1, fetched[chunk + 1], gather(f"y{chunk + 1}", fetched[chunk + 1]))
        work(chunk)
        reduce(chunk)
        if chunk > 0:
            give(chunk - 1)
    give(chunks - 1)
    return combine_rows(target, route_gates, returned, slot)


def solution(mesh):
    in_specs = (
        P("ep", "tp"),
        P("ep", None),
        P("ep", None),
        P("ep", None, "tp"),
        P("ep", "tp", None),
    )
    out_specs = P("ep", "tp")
    return jax.shard_map(
        per_device, mesh=mesh, in_specs=in_specs, out_specs=out_specs, check_vma=False
    )
```
